32 devices in a mesh: grp: 2 (over x), patch: 8 (over z, y), head: 2 (over core).
Axes of the slice: x: 2, y: 2, z: 4, core: 2. Of those that a mesh axis runs over, the one named last changes fastest.
Arguments:
- queries: bfloat16 [4096, 1536], P(('grp', 'patch'), 'head'), parts along dimension 0, as said below
- fresh_pairs: bfloat16 [2, 4096, 1536], P(None, ('grp', 'patch'), 'head'), parts along dimension 1, may hold values from -5 to 5
- stale_pairs: bfloat16 [2, 2304, 1536], P(None, ('grp', 'patch'), 'head'), parts along dimension 1, as said below
- counts: int32 [16], P('grp'), parts along dimension 0, may hold values from 1 to 256, 1152 in all
- latents: bfloat16 [4096, 3072], P(('grp', 'patch'), 'head'), parts along dimension 0, may hold values from -6 to 6
- out_weight: bfloat16 [1536, 3072], P('head'), may hold values from -0.3125 to 0.3125
- gate: bfloat16 [6144], P(('grp', 'head')), parts along dimension 0, may hold values from 0.5 to 2
Outputs:
- mixed: bfloat16 [4096, 3072], P(('grp', 'patch'), 'head'), parts along dimension 0
The draws below stay inside these ranges and needn't reach their ends.
There are 2 independent parts, one for each index of `grp`. The reference program is written for one: setup_inputs(seed, part) draws one part's arguments, and reference() takes and returns one part's arrays. A program takes and returns all parts, laid end to end along the dimension named above; an argument that names none is the same for every part. Nothing has to cross between parts.
Inputs may be any that keep to these rules, and one draw needn't show every extreme that they name: `queries`: every entry lies within -160 and 160. `stale_pairs`: every entry lies within -6 and 6. Device p of the patch axis holds live tokens in its first counts[p] slots; the counts sum to 1152.
All inputs are finite; a program needn't handle non-finite values.
Results may differ from the reference program's by a relative error of at most 0.009.
Values may be sent and summed in bfloat16 or wider, within the bound.
A program may use at most 192 MiB of HBM per device.

```python
import math
import jax
import jax.numpy as jnp
import numpy as np
from jax import lax

D = 3072
HEADS = 12
HEAD_DIM = 128
SLOTS = 256
TOTAL = 1152
SPAN = 2048
N_PATCH = 8


def shared_keys(key):
    base = jax.random.normal(jax.random.fold_in(key, 7), (TOTAL, HEADS * HEAD_DIM), jnp.float32)
    return jnp.clip(base, -5.0, 5.0)


def draw_queries(key, part):
    key = jax.random.fold_in(key, 4)
    drawn = 3.0 * jnp.clip(jax.random.normal(key, (SPAN, HEADS * HEAD_DIM), jnp.float32), -5.0, 5.0)
    return drawn.astype(jnp.bfloat16)


def draw_stale_pairs(key, part):
    base = shared_keys(key)
    key = jax.random.fold_in(key, 3)
    values = jnp.clip(jax.random.normal(key, (TOTAL, HEADS * HEAD_DIM), jnp.float32), -5.0, 5.0)
    keys = base
    return jnp.stack([keys, values]).astype(jnp.bfloat16)


def block_levels(rng, shape, pieces, least, largest):
    loudness = 1.0
    for dim, shards_of in pieces:
        steps = jax.random.uniform(jax.random.fold_in(jax.random.fold_in(rng, 6), dim), (shards_of,), jnp.float32, least / len(pieces), largest / len(pieces))
        loudness = loudness * jnp.repeat(jnp.exp(steps), shape[dim] // shards_of).reshape((-1,) + (1,) * (len(shape) - 1 - dim))
    return loudness


def profile(count, total, reach, lean):
    weights = [(1 << 20) // math.isqrt(grade ** lean) + 1 for grade in range(2, count + 1)]
    spare, holding = total - reach - (count - 1), [1] * (count - 1)
    while spare > 0:
        candidates = [i for i in range(count - 1) if holding[i] < reach]
        pool, budget = sum([weights[i] for i in candidates]), spare
        for i in candidates:
            more = min(reach - holding[i], max(1, budget * weights[i] // pool), spare)
            holding[i] = holding[i] + more
            spare = spare - more
    return np.array([reach] + holding)


def ragged(key, number_of, total, most, lean):
    if number_of == 2:
        one = jax.random.randint(key, (), max(1, total - most), min(most, total - 1) + 1)
        return jnp.stack([one, total - one])
    sizes = jnp.asarray(profile(number_of, total, most, lean), jnp.int32)
    pairs = (number_of - 1) // 2
    source_of, receiver = sizes[1:1 + 2 * pairs:2], sizes[2:2 + 2 * pairs:2]
    margin = jnp.minimum(source_of - 1, most - receiver)
    moved = jax.random.randint(jax.random.fold_in(key, 1), (pairs,), 0, 1 << 20) % (margin + 1)
    sizes = sizes.at[1:1 + 2 * pairs:2].set(source_of - moved).at[2:2 + 2 * pairs:2].set(receiver + moved)
    return sizes[jax.random.permutation(jax.random.fold_in(key, 2), number_of)]


def normal_values(rng, shape, width, reach, cuts=(), held_as=jnp.bfloat16):
    entries = width * jax.random.normal(rng, shape, jnp.float32)
    if cuts:
        entries = entries * block_levels(rng, shape, cuts, -0.22, 0.18)
    return jnp.clip(entries, -reach, reach).astype(held_as)


def setup_inputs(seed: int = 0, part: int = 0) -> dict:
    key_list = jax.random.split(jax.random.key(seed), 8)
    part_keys = jax.random.split(jax.random.fold_in(key_list[7], part), 8)
    return {
        "queries": draw_queries(jax.random.fold_in(jax.random.fold_in(key_list[7], part), 71), part),
        "fresh_pairs": normal_values(part_keys[1], (2, SPAN, HEADS * HEAD_DIM), 1.0, 5.0, ((1, 8), (2, 2))),
        "stale_pairs": draw_stale_pairs(jax.random.fold_in(jax.random.fold_in(key_list[7], part), 71), part),
        "counts": ragged(part_keys[3], N_PATCH, TOTAL, SLOTS, 2).astype(jnp.int32),
        "latents": normal_values(part_keys[4], (SPAN, D), 1.0, 6.0, ((0, 8), (1, 2))),
        "out_weight": normal_values(key_list[5], (HEADS * HEAD_DIM, D), (HEADS * HEAD_DIM // 4) ** -0.5, 0.3125, ((0, 2),)),
        "gate": jnp.clip(0.5 + 1.5 * jax.random.uniform(part_keys[6], (D,), jnp.float32) ** block_levels(part_keys[6], (D,), ((0, 2),), -0.2, 0.2), 0.5, 2.0).astype(jnp.bfloat16),
    }


masked_score = -1e30


def reference(queries, fresh_pairs, stale_pairs, counts, latents, out_weight, gate):
    counts = counts.astype(jnp.int32)
    offsets = (jnp.cumsum(counts) - counts).astype(jnp.int32)
    key_rows = jnp.arange(TOTAL, dtype=jnp.int32)
    slot_rows = jnp.arange(SLOTS, dtype=jnp.int32)
    factor = 1.0 / float(HEAD_DIM) ** 0.5
    stale = stale_pairs.astype(jnp.float32)

    def one_owner(owner):
        start = (owner * SLOTS).astype(jnp.int32)
        query = lax.dynamic_slice_in_dim(queries, start, SLOTS, 0).astype(jnp.float32)
        query = query.reshape(SLOTS, HEADS, HEAD_DIM)
        fresh = lax.dynamic_slice_in_dim(fresh_pairs, start, SLOTS, 1).astype(jnp.float32)
        own_live = slot_rows < counts[owner]
        low = offsets[owner]
        high = low + counts[owner]
        stale_live = (key_rows < low) | (key_rows >= high)
        live = jnp.concatenate([own_live, stale_live])
        keys = jnp.concatenate([fresh[0], stale[0]], axis=0).reshape(SLOTS + TOTAL, HEADS, HEAD_DIM)
        values = jnp.concatenate([fresh[1], stale[1]], axis=0).reshape(SLOTS + TOTAL, HEADS, HEAD_DIM)
        scores = jnp.einsum("qhd,khd->hqk", query, keys) * factor
        scores = jnp.where(live[None, None, :], scores, masked_score)
        top = jnp.max(scores, axis=-1, keepdims=True)
        weights = jnp.exp(scores - top)
        total = jnp.sum(weights, axis=-1)
        rounded = weights.astype(jnp.bfloat16).astype(jnp.float32)
        summed = jnp.einsum("hqk,khd->hqd", rounded, values)
        attended = summed / total[:, :, None]
        return attended.transpose(1, 0, 2).reshape(SLOTS, HEADS * HEAD_DIM).astype(jnp.bfloat16)

    attended = lax.map(one_owner, jnp.arange(N_PATCH, dtype=jnp.int32))
    attended = attended.reshape(SPAN, HEADS * HEAD_DIM)
    projected = jnp.dot(attended, out_weight, preferred_element_type=jnp.float32)
    mixed = latents.astype(jnp.float32) + gate.astype(jnp.float32)[None, :] * projected
    return mixed.astype(jnp.bfloat16)
```

```python
import functools
import math

import jax
import jax.numpy as jnp
from jax import lax
from jax.experimental import pallas as pl
from jax.experimental.pallas import tpu as pltpu
from jax.sharding import PartitionSpec as P

HEAD_DIM = 128
MASKED = -1e30
MESH = pl.DeviceIdType.MESH


def kernel(
    n, inner, counts_ref, q_hbm, fresh_hbm, stale_hbm, lat_hbm, w_hbm, gate_ref, out_hbm,
    q, fresh, slots, lat, w_own, w_other, top, total, acc, att_own, att_other, proj, mixed,
    local_sem, send_sem, recv_sem, w_sem, att_send, att_recv, out_sem,
):
    Z, Y = n // inner, inner
    grp, me, core = lax.axis_index("grp"), lax.axis_index("patch"), lax.axis_index("head")
    z, y = me // Y, me % Y
    rows = slots.shape[2]
    width = q.shape[1]
    heads = width // HEAD_DIM
    half = lat.shape[1]
    scale = math.log2(math.e) / HEAD_DIM ** 0.5
    cut = (rows // 3) // 16 * 16
    pieces = ((0, 0, rows, False), (1, cut, rows - cut, False), (1, 0, cut, True))
    other = (grp, me, 1 - core)

    def there(step):
        return (grp, me + step, core)

    sides = ((z > 0, -Y), (z < Z - 1, Y), (y > 0, -1), (y < Y - 1, 1))

    own_copy = pltpu.make_async_copy(stale_hbm, slots.at[me], local_sem.at[0])
    own_copy.start()
    q_copy = pltpu.make_async_copy(q_hbm, q, local_sem.at[1])
    q_copy.start()
    fresh_copy = pltpu.make_async_copy(fresh_hbm, fresh, local_sem.at[2])
    fresh_copy.start()

    barrier = pltpu.get_barrier_semaphore()
    for there_is, step in sides:
        @pl.when(there_is)
        def _():
            pl.semaphore_signal(barrier, inc=1, device_id=there(step), device_id_type=MESH)
    pl.semaphore_signal(barrier, inc=1, device_id=other, device_id_type=MESH)
    peers = jnp.int32(1)
    for there_is, _step in sides:
        peers = peers + there_is.astype(jnp.int32)
    pl.semaphore_wait(barrier, peers)

    def piece_copy(slot, k, side):
        kind, first, count, _ = pieces[k]
        ref = slots.at[slot, kind, pl.ds(first, count), :]
        return pltpu.make_async_remote_copy(
            src_ref=ref, dst_ref=ref, send_sem=send_sem.at[k, side, slot],
            recv_sem=recv_sem.at[k, slot], device_id=there(sides[side][1]), device_id_type=MESH,
        )

    def sends(zs, ys, k):
        y_first = pieces[k][3]
        down, up = (zs >= z) & (z > 0), (zs <= z) & (z < Z - 1)
        left, right = (ys >= y) & (y > 0), (ys <= y) & (y < Y - 1)
        if y_first:
            return down, up, left & (zs == z), right & (zs == z)
        return down & (ys == y), up & (ys == y), left, right

    def forward(zs, ys, k):
        slot = zs * Y + ys
        for side, goes in enumerate(sends(zs, ys, k)):
            @pl.when(goes)
            def _():
                piece_copy(slot, k, side).start()

    def arrive(zs, ys, k):
        piece_copy(zs * Y + ys, k, 0).wait_recv()
        forward(zs, ys, k)

    own_copy.wait()
    for k in range(3):
        forward(z, y, k)

    lat_copy = pltpu.make_async_copy(lat_hbm, lat, local_sem.at[3])
    lat_copy.start()
    mine = pl.ds(pl.multiple_of(core * half, half), half)
    theirs = pl.ds(pl.multiple_of((1 - core) * half, half), half)
    w_copy = pltpu.make_async_copy(w_hbm.at[:, mine], w_own, local_sem.at[4])
    w_copy.start()
    w_send = pltpu.make_async_remote_copy(
        src_ref=w_hbm.at[:, theirs], dst_ref=w_other, send_sem=w_sem.at[0], recv_sem=w_sem.at[1],
        device_id=other, device_id_type=MESH,
    )
    w_send.start()

    low = jnp.int32(0)
    own = jnp.int32(0)
    for p in range(n):
        count = counts_ref[p]
        low = low + jnp.where(p < me, count, 0)
        own = own + jnp.where(p == me, count, 0)
    high = low + own

    def part(key_of, value_of, dead, first):
        for h in range(heads):
            at = slice(h * HEAD_DIM, (h + 1) * HEAD_DIM)
            s = lax.dot_general(
                key_of(at), q[:, at], (((1,), (1,)), ((), ())), preferred_element_type=jnp.float32
            )
            s = jnp.where(dead, MASKED, s)
            peak = jnp.max(s, axis=0, keepdims=True)
            if not first:
                before = top[h]
                peak = jnp.maximum(before, peak)
            weights = jnp.exp2((s - peak) * scale)
            summed = jnp.sum(weights, axis=0, keepdims=True)
            added = lax.dot_general(
                value_of(at), weights.astype(jnp.bfloat16), (((0,), (0,)), ((), ())),
                preferred_element_type=jnp.float32,
            )
            top[h] = peak
            if first:
                total[h] = summed
                acc[h] = added
            else:
                shrink = jnp.exp2((before - peak) * scale)
                total[h] = total[h] * shrink + summed
                acc[h] = acc[h] * shrink + added

    def attend(zs, ys):
        slot = zs * Y + ys
        row = slot * rows + lax.broadcasted_iota(jnp.int32, (rows, q.shape[0]), 0)
        dead = (row >= low) & (row < high)
        part(lambda at: slots[slot, 0, :, at], lambda at: slots[slot, 1, :, at], dead, False)

    q_copy.wait()
    fresh_copy.wait()
    place = lax.broadcasted_iota(jnp.int32, (fresh.shape[1], q.shape[0]), 0)
    part(lambda at: fresh[0, :, at], lambda at: fresh[1, :, at], place >= own, True)

    def step(d, carry):
        for k in range(3):
            for sign in (-1, 1):
                zs = z + sign * d

                @pl.when((d >= 1) & (zs >= 0) & (zs < Z))
                def _():
                    arrive(zs, y, k)

        e = d - 1

        def along_y(t, carry):
            dy, sz, sy = t // 4 + 1, 2 * ((t // 2) % 2) - 1, 2 * (t % 2) - 1
            zs, ys = z + sz * e, y + sy * dy
            once = (e >= 1) | ((e == 0) & (sz == 1))

            @pl.when(once & (zs >= 0) & (zs < Z) & (ys >= 0) & (ys < Y))
            def _():
                for k in range(3):
                    arrive(zs, ys, k)
                attend(zs, ys)
            return carry

        lax.fori_loop(0, 4 * (Y - 1), along_y, 0)

        def along_z(t, carry):
            zs = z + (2 * t - 1) * d

            @pl.when(((d >= 1) | (t == 1)) & (zs >= 0) & (zs < Z))
            def _():
                attend(zs, y)
            return carry

        lax.fori_loop(0, 2, along_z, 0)
        return carry

    lax.fori_loop(0, Z + 1, step, 0)

    def att_copy(h):
        at = pl.ds(h * HEAD_DIM, HEAD_DIM)
        return pltpu.make_async_remote_copy(
            src_ref=att_own.at[:, at], dst_ref=att_other.at[:, at], send_sem=att_send.at[h],
            recv_sem=att_recv.at[h], device_id=other, device_id_type=MESH,
        )

    for h in range(heads):
        done = acc[h] / total[h]
        att_own[:, h * HEAD_DIM:(h + 1) * HEAD_DIM] = done.T.astype(jnp.bfloat16)
        att_copy(h).start()

    w_copy.wait()
    chunk = half // 3
    for c in range(3):
        at = slice(c * chunk, (c + 1) * chunk)
        proj[:, at] = jnp.dot(att_own[...], w_own[:, at], preferred_element_type=jnp.float32)
    lat_copy.wait()
    w_send.wait()
    for h in range(heads):
        att_copy(h).wait()
    outs = []
    for c in range(3):
        at = slice(c * chunk, (c + 1) * chunk)
        full = proj[:, at] + jnp.dot(
            att_other[...], w_other[:, at], preferred_element_type=jnp.float32
        )
        result = lat[:, at].astype(jnp.float32) + gate_ref[:, at].astype(jnp.float32) * full
        mixed[:, at] = result.astype(jnp.bfloat16)
        there_at = pl.ds(c * chunk, chunk)
        copy = pltpu.make_async_copy(mixed.at[:, there_at], out_hbm.at[:, there_at], out_sem.at[c])
        copy.start()
        outs.append(copy)

    def sent(slot, carry):
        zs, ys = slot // Y, slot % Y
        for k in range(3):
            for side, goes in enumerate(sends(zs, ys, k)):
                @pl.when(goes)
                def _():
                    piece_copy(slot, k, side).wait_send()
        return carry

    lax.fori_loop(0, n, sent, 0)
    for copy in outs:
        copy.wait()


def local(n, inner, queries, fresh_pairs, stale_pairs, counts, latents, out_weight, gate):
    slots, width = queries.shape
    rows = stale_pairs.shape[1]
    half = latents.shape[1]
    heads = width // HEAD_DIM
    bf16, f32 = jnp.bfloat16, jnp.float32
    anywhere = pl.BlockSpec(memory_space=pl.ANY)
    dma = pltpu.SemaphoreType.DMA
    return pl.pallas_call(
        functools.partial(kernel, n, inner),
        out_shape=jax.ShapeDtypeStruct((slots, half), bf16),
        in_specs=[pl.BlockSpec(memory_space=pltpu.SMEM)] + [anywhere] * 5
        + [pl.BlockSpec(memory_space=pltpu.VMEM)],
        out_specs=anywhere,
        scratch_shapes=[
            pltpu.VMEM((slots, width), bf16),
            pltpu.VMEM((2, slots, width), bf16),
            pltpu.VMEM((n, 2, rows, width), bf16),
            pltpu.VMEM((slots, half), bf16),
            pltpu.VMEM((width, half), bf16),
            pltpu.VMEM((width, half), bf16),
            pltpu.VMEM((heads, 1, slots), f32),
            pltpu.VMEM((heads, 1, slots), f32),
            pltpu.VMEM((heads, HEAD_DIM, slots), f32),
            pltpu.VMEM((slots, width), bf16),
            pltpu.VMEM((slots, width), bf16),
            pltpu.VMEM((slots, half), f32),
            pltpu.VMEM((slots, half), bf16),
            dma((5,)),
            dma((3, 4, n)),
            dma((3, n)),
            dma((2,)),
            dma((heads,)),
            dma((heads,)),
            dma((3,)),
        ],
        compiler_params=pltpu.CompilerParams(
            collective_id=0, has_side_effects=True, vmem_limit_bytes=56 * 2 ** 20
        ),
    )(counts, queries, fresh_pairs, stale_pairs, latents, out_weight, gate.reshape(1, -1))


def solution(mesh):
    n = mesh.shape["patch"]
    root = math.isqrt(n)
    inner = next(size for size in range(root, 0, -1) if n % size == 0)
    placed = (
        P(("grp", "patch"), "head"),
        P(None, ("grp", "patch"), "head"),
        P(None, ("grp", "patch"), "head"),
        P("grp"),
        P(("grp", "patch"), "head"),
        P("head", None),
        P(("grp", "head")),
    )
    return jax.shard_map(
        functools.partial(local, n, inner), mesh=mesh, in_specs=placed,
        out_specs=P(("grp", "patch"), "head"), check_vma=False,
    )
```

```python
import functools
import math

import jax
import jax.numpy as jnp
from jax import lax
from jax.experimental import pallas as pl
from jax.experimental.pallas import tpu as pltpu
from jax.sharding import PartitionSpec as P

HEAD_DIM = 128
MASKED = -1e30
MESH = pl.DeviceIdType.MESH


def kernel(
    n, inner, counts_ref, q_hbm, fresh_hbm, stale_hbm, lat_hbm, w_hbm, gate_ref, out_hbm,
    q, fresh, slots, lat, w_own, w_other, top, total, acc, att_own, att_other, proj, mixed,
    local_sem, send_sem, recv_sem, w_sem, att_send, att_recv, out_sem,
):
    Z, Y = n // inner, inner
    grp, me, core = lax.axis_index("grp"), lax.axis_index("patch"), lax.axis_index("head")
    z, y = me // Y, me % Y
    rows = slots.shape[2]
    width = q.shape[1]
    heads = width // HEAD_DIM
    half = lat.shape[1]
    scale = math.log2(math.e) / HEAD_DIM ** 0.5
    cut = (rows // 3) // 16 * 16
    pieces = ((0, 0, rows, False), (1, cut, rows - cut, False), (1, 0, cut, True))
    other = (grp, me, 1 - core)

    def there(step):
        return (grp, me + step, core)

    sides = ((z > 0, -Y), (z < Z - 1, Y), (y > 0, -1), (y < Y - 1, 1))

    own_copy = pltpu.make_async_copy(stale_hbm, slots.at[me], local_sem.at[0])
    own_copy.start()
    q_copy = pltpu.make_async_copy(q_hbm, q, local_sem.at[1])
    q_copy.start()
    fresh_copy = pltpu.make_async_copy(fresh_hbm, fresh, local_sem.at[2])
    fresh_copy.start()

    barrier = pltpu.get_barrier_semaphore()
    for there_is, step in sides:
        @pl.when(there_is)
        def _():
            pl.semaphore_signal(barrier, inc=1, device_id=there(step), device_id_type=MESH)
    pl.semaphore_signal(barrier, inc=1, device_id=other, device_id_type=MESH)
    peers = jnp.int32(1)
    for there_is, _step in sides:
        peers = peers + there_is.astype(jnp.int32)
    pl.semaphore_wait(barrier, peers)

    def piece_copy(slot, k, side):
        kind, first, count, _ = pieces[k]
        ref = slots.at[slot, kind, pl.ds(first, count), :]
        return pltpu.make_async_remote_copy(
            src_ref=ref, dst_ref=ref, send_sem=send_sem.at[k, side, slot],
            recv_sem=recv_sem.at[k, slot], device_id=there(sides[side][1]), device_id_type=MESH,
        )

    def sends(zs, ys, k):
        y_first = pieces[k][3]
        down, up = (zs >= z) & (z > 0), (zs <= z) & (z < Z - 1)
        left, right = (ys >= y) & (y > 0), (ys <= y) & (y < Y - 1)
        if y_first:
            return down, up, left & (zs == z), right & (zs == z)
        return down & (ys == y), up & (ys == y), left, right

    def forward(zs, ys, k):
        slot = zs * Y + ys
        for side, goes in enumerate(sends(zs, ys, k)):
            @pl.when(goes)
            def _():
                piece_copy(slot, k, side).start()

    def arrive(zs, ys, k):
        piece_copy(zs * Y + ys, k, 0).wait_recv()
        forward(zs, ys, k)

    own_copy.wait()
    for k in range(3):
        forward(z, y, k)

    lat_copy = pltpu.make_async_copy(lat_hbm, lat, local_sem.at[3])
    lat_copy.start()
    mine = pl.ds(pl.multiple_of(core * half, half), half)
    theirs = pl.ds(pl.multiple_of((1 - core) * half, half), half)
    w_copy = pltpu.make_async_copy(w_hbm.at[:, mine], w_own, local_sem.at[4])
    w_copy.start()
    w_send = pltpu.make_async_remote_copy(
        src_ref=w_hbm.at[:, theirs], dst_ref=w_other, send_sem=w_sem.at[0], recv_sem=w_sem.at[1],
        device_id=other, device_id_type=MESH,
    )
    w_send.start()

    low = jnp.int32(0)
    own = jnp.int32(0)
    for p in range(n):
        count = counts_ref[p]
        low = low + jnp.where(p < me, count, 0)
        own = own + jnp.where(p == me, count, 0)
    high = low + own

    def part(key_of, value_of, dead, first):
        for h in range(heads):
            at = slice(h * HEAD_DIM, (h + 1) * HEAD_DIM)
            s = lax.dot_general(
                key_of(at), q[:, at], (((1,), (1,)), ((), ())), preferred_element_type=jnp.float32
            )
            s = jnp.where(dead, MASKED, s)
            peak = jnp.max(s, axis=0, keepdims=True)
            if not first:
                before = top[h]
                peak = jnp.maximum(before, peak)
            weights = jnp.exp2((s - peak) * scale)
            summed = jnp.sum(weights, axis=0, keepdims=True)
            added = lax.dot_general(
                value_of(at), weights.astype(jnp.bfloat16), (((0,), (0,)), ((), ())),
                preferred_element_type=jnp.float32,
            )
            top[h] = peak
            if first:
                total[h] = summed
                acc[h] = added
            else:
                shrink = jnp.exp2((before - peak) * scale)
                total[h] = total[h] * shrink + summed
                acc[h] = acc[h] * shrink + added

    def attend(zs, ys):
        slot = zs * Y + ys
        row = slot * rows + lax.broadcasted_iota(jnp.int32, (rows, q.shape[0]), 0)
        dead = (row >= low) & (row < high)
        part(lambda at: slots[slot, 0, :, at], lambda at: slots[slot, 1, :, at], dead, False)

    q_copy.wait()
    fresh_copy.wait()
    place = lax.broadcasted_iota(jnp.int32, (fresh.shape[1], q.shape[0]), 0)
    part(lambda at: fresh[0, :, at], lambda at: fresh[1, :, at], place >= own, True)

    def step(d, carry):
        for k in range(3):
            for sign in (-1, 1):
                zs = z + sign * d

                @pl.when((d >= 1) & (zs >= 0) & (zs < Z))
                def _():
                    arrive(zs, y, k)

        e = d - 1

        def along_y(t, carry):
            dy, sz, sy = t // 4 + 1, 2 * ((t // 2) % 2) - 1, 2 * (t % 2) - 1
            zs, ys = z + sz * e, y + sy * dy
            once = (e >= 1) | ((e == 0) & (sz == 1))

            @pl.when(once & (zs >= 0) & (zs < Z) & (ys >= 0) & (ys < Y))
            def _():
                for k in range(3):
                    arrive(zs, ys, k)
                attend(zs, ys)
            return carry

        lax.fori_loop(0, 4 * (Y - 1), along_y, 0)

        def along_z(t, carry):
            zs = z + (2 * t - 1) * d

            @pl.when(((d >= 1) | (t == 1)) & (zs >= 0) & (zs < Z))
            def _():
                attend(zs, y)
            return carry

        lax.fori_loop(0, 2, along_z, 0)
        return carry

    lax.fori_loop(0, Z + 1, step, 0)

    def att_copy(h):
        at = pl.ds(h * HEAD_DIM, HEAD_DIM)
        return pltpu.make_async_remote_copy(
            src_ref=att_own.at[:, at], dst_ref=att_other.at[:, at], send_sem=att_send.at[h],
            recv_sem=att_recv.at[h], device_id=other, device_id_type=MESH,
        )

    for h in range(heads):
        done = acc[h] / total[h]
        att_own[:, h * HEAD_DIM:(h + 1) * HEAD_DIM] = done.T.astype(jnp.bfloat16)
        att_copy(h).start()

    w_copy.wait()
    chunk = half // 3
    for c in range(3):
        at = slice(c * chunk, (c + 1) * chunk)
        proj[:, at] = jnp.dot(att_own[...], w_own[:, at], preferred_element_type=jnp.float32)
    lat_copy.wait()
    w_send.wait()
    for h in range(heads):
        att_copy(h).wait()
    outs = []
    for c in range(3):
        at = slice(c * chunk, (c + 1) * chunk)
        full = proj[:, at] + jnp.dot(
            att_other[...], w_other[:, at], preferred_element_type=jnp.float32
        )
        result = lat[:, at].astype(jnp.float32) + gate_ref[at].astype(jnp.float32)[None, :] * full
        mixed[:, at] = result.astype(jnp.bfloat16)
        there_at = pl.ds(c * chunk, chunk)
        copy = pltpu.make_async_copy(mixed.at[:, there_at], out_hbm.at[:, there_at], out_sem.at[c])
        copy.start()
        outs.append(copy)

    def sent(slot, carry):
        zs, ys = slot // Y, slot % Y
        for k in range(3):
            for side, goes in enumerate(sends(zs, ys, k)):
                @pl.when(goes)
                def _():
                    piece_copy(slot, k, side).wait_send()
        return carry

    lax.fori_loop(0, n, sent, 0)
    for copy in outs:
        copy.wait()


def local(n, inner, queries, fresh_pairs, stale_pairs, counts, latents, out_weight, gate):
    slots, width = queries.shape
    rows = stale_pairs.shape[1]
    half = latents.shape[1]
    heads = width // HEAD_DIM
    bf16, f32 = jnp.bfloat16, jnp.float32
    anywhere = pl.BlockSpec(memory_space=pl.ANY)
    dma = pltpu.SemaphoreType.DMA
    return pl.pallas_call(
        functools.partial(kernel, n, inner),
        out_shape=jax.ShapeDtypeStruct((slots, half), bf16),
        in_specs=[pl.BlockSpec(memory_space=pltpu.SMEM)] + [anywhere] * 5
        + [pl.BlockSpec(memory_space=pltpu.VMEM)],
        out_specs=anywhere,
        scratch_shapes=[
            pltpu.VMEM((slots, width), bf16),
            pltpu.VMEM((2, slots, width), bf16),
            pltpu.VMEM((n, 2, rows, width), bf16),
            pltpu.VMEM((slots, half), bf16),
            pltpu.VMEM((width, half), bf16),
            pltpu.VMEM((width, half), bf16),
            pltpu.VMEM((heads, 1, slots), f32),
            pltpu.VMEM((heads, 1, slots), f32),
            pltpu.VMEM((heads, HEAD_DIM, slots), f32),
            pltpu.VMEM((slots, width), bf16),
            pltpu.VMEM((slots, width), bf16),
            pltpu.VMEM((slots, half), f32),
            pltpu.VMEM((slots, half), bf16),
            dma((5,)),
            dma((3, 4, n)),
            dma((3, n)),
            dma((2,)),
            dma((heads,)),
            dma((heads,)),
            dma((3,)),
        ],
        compiler_params=pltpu.CompilerParams(
            collective_id=0, has_side_effects=True, vmem_limit_bytes=56 * 2 ** 20
        ),
    )(counts, queries, fresh_pairs, stale_pairs, latents, out_weight, gate)


def solution(mesh):
    n = mesh.shape["patch"]
    root = math.isqrt(n)
    inner = next(size for size in range(root, 0, -1) if n % size == 0)
    placed = (
        P(("grp", "patch"), "head"),
        P(None, ("grp", "patch"), "head"),
        P(None, ("grp", "patch"), "head"),
        P("grp"),
        P(("grp", "patch"), "head"),
        P("head", None),
        P(("grp", "head")),
    )
    return jax.shard_map(
        functools.partial(local, n, inner), mesh=mesh, in_specs=placed,
        out_specs=P(("grp", "patch"), "head"), check_vma=False,
    )
```

```python
import functools
import math

import jax
import jax.numpy as jnp
from jax import lax
from jax.experimental import pallas as pl
from jax.experimental.pallas import tpu as pltpu
from jax.sharding import PartitionSpec as P

HEAD_DIM = 128
MASKED = -1e30
MESH = pl.DeviceIdType.MESH


def kernel(
    n, inner, counts_ref, q_hbm, fresh_hbm, stale_hbm, lat_hbm, w_hbm, gate_ref, out_hbm,
    q, fresh, slots, lat, w_own, w_other, top, total, acc, att_own, att_other, proj, mixed,
    local_sem, send_sem, recv_sem, w_sem, att_send, att_recv, out_sem,
):
    Z, Y = n // inner, inner
    grp, me, core = lax.axis_index("grp"), lax.axis_index("patch"), lax.axis_index("head")
    z, y = me // Y, me % Y
    rows = slots.shape[2]
    width = q.shape[1]
    heads = width // HEAD_DIM
    half = lat.shape[1]
    scale = math.log2(math.e) / HEAD_DIM ** 0.5
    cut = (rows // 3) // 16 * 16
    pieces = ((1, 0, cut, True), (0, 0, cut, False), (0, cut, cut, False), (0, 2 * cut, rows - 2 * cut, False), (1, cut, cut, False), (1, 2 * cut, rows - 2 * cut, False))
    other = (grp, me, 1 - core)

    def there(step):
        return (grp, me + step, core)

    sides = ((z > 0, -Y), (z < Z - 1, Y), (y > 0, -1), (y < Y - 1, 1))

    own_copy = pltpu.make_async_copy(stale_hbm, slots.at[me], local_sem.at[0])
    own_copy.start()
    q_copy = pltpu.make_async_copy(q_hbm, q, local_sem.at[1])
    q_copy.start()
    fresh_copy = pltpu.make_async_copy(fresh_hbm, fresh, local_sem.at[2])
    fresh_copy.start()

    barrier = pltpu.get_barrier_semaphore()
    for there_is, step in sides:
        @pl.when(there_is)
        def _():
            pl.semaphore_signal(barrier, inc=1, device_id=there(step), device_id_type=MESH)
    pl.semaphore_signal(barrier, inc=1, device_id=other, device_id_type=MESH)
    peers = jnp.int32(1)
    for there_is, _step in sides:
        peers = peers + there_is.astype(jnp.int32)
    pl.semaphore_wait(barrier, peers)

    def piece_copy(slot, k, side):
        kind, first, count, _ = pieces[k]
        ref = slots.at[slot, kind, pl.ds(first, count), :]
        return pltpu.make_async_remote_copy(
            src_ref=ref, dst_ref=ref, send_sem=send_sem.at[k, side, slot],
            recv_sem=recv_sem.at[k, slot], device_id=there(sides[side][1]), device_id_type=MESH,
        )

    def sends(zs, ys, k):
        y_first = pieces[k][3]
        down, up = (zs >= z) & (z > 0), (zs <= z) & (z < Z - 1)
        left, right = (ys >= y) & (y > 0), (ys <= y) & (y < Y - 1)
        if y_first:
            return down, up, left & (zs == z), right & (zs == z)
        return down & (ys == y), up & (ys == y), left, right

    def forward(zs, ys, k):
        slot = zs * Y + ys
        for side, goes in enumerate(sends(zs, ys, k)):
            @pl.when(goes)
            def _():
                piece_copy(slot, k, side).start()

    def arrive(zs, ys, k):
        piece_copy(zs * Y + ys, k, 0).wait_recv()
        forward(zs, ys, k)

    own_copy.wait()
    for k in range(len(pieces)):
        forward(z, y, k)

    lat_copy = pltpu.make_async_copy(lat_hbm, lat, local_sem.at[3])
    lat_copy.start()
    mine = pl.ds(pl.multiple_of(core * half, half), half)
    theirs = pl.ds(pl.multiple_of((1 - core) * half, half), half)
    w_copy = pltpu.make_async_copy(w_hbm.at[:, mine], w_own, local_sem.at[4])
    w_copy.start()
    w_send = pltpu.make_async_remote_copy(
        src_ref=w_hbm.at[:, theirs], dst_ref=w_other, send_sem=w_sem.at[0], recv_sem=w_sem.at[1],
        device_id=other, device_id_type=MESH,
    )
    w_send.start()

    low = jnp.int32(0)
    own = jnp.int32(0)
    for p in range(n):
        count = counts_ref[p]
        low = low + jnp.where(p < me, count, 0)
        own = own + jnp.where(p == me, count, 0)
    high = low + own

    def part(key_of, value_of, dead, first):
        for h in range(heads):
            at = slice(h * HEAD_DIM, (h + 1) * HEAD_DIM)
            s = lax.dot_general(
                key_of(at), q[:, at], (((1,), (1,)), ((), ())), preferred_element_type=jnp.float32
            )
            s = jnp.where(dead, MASKED, s)
            peak = jnp.max(s, axis=0, keepdims=True)
            if not first:
                before = top[h]
                peak = jnp.maximum(before, peak)
            weights = jnp.exp2((s - peak) * scale)
            summed = jnp.sum(weights, axis=0, keepdims=True)
            added = lax.dot_general(
                value_of(at), weights.astype(jnp.bfloat16), (((0,), (0,)), ((), ())),
                preferred_element_type=jnp.float32,
            )
            top[h] = peak
            if first:
                total[h] = summed
                acc[h] = added
            else:
                shrink = jnp.exp2((before - peak) * scale)
                total[h] = total[h] * shrink + summed
                acc[h] = acc[h] * shrink + added

    def attend(zs, ys):
        slot = zs * Y + ys
        row = slot * rows + lax.broadcasted_iota(jnp.int32, (rows, q.shape[0]), 0)
        dead = (row >= low) & (row < high)
        part(lambda at: slots[slot, 0, :, at], lambda at: slots[slot, 1, :, at], dead, False)

    q_copy.wait()
    fresh_copy.wait()
    place = lax.broadcasted_iota(jnp.int32, (fresh.shape[1], q.shape[0]), 0)
    part(lambda at: fresh[0, :, at], lambda at: fresh[1, :, at], place >= own, True)

    def step(d, carry):
        for k in range(len(pieces)):
            for sign in (-1, 1):
                zs = z + sign * d

                @pl.when((d >= 1) & (zs >= 0) & (zs < Z))
                def _():
                    arrive(zs, y, k)

        e = d - 1

        def along_y(t, carry):
            dy, sz, sy = t // 4 + 1, 2 * ((t // 2) % 2) - 1, 2 * (t % 2) - 1
            zs, ys = z + sz * e, y + sy * dy
            once = (e >= 1) | ((e == 0) & (sz == 1))

            @pl.when(once & (zs >= 0) & (zs < Z) & (ys >= 0) & (ys < Y))
            def _():
                for k in range(len(pieces)):
                    arrive(zs, ys, k)
                attend(zs, ys)
            return carry

        lax.fori_loop(0, 4 * (Y - 1), along_y, 0)

        def along_z(t, carry):
            zs = z + (2 * t - 1) * d

            @pl.when(((d >= 1) | (t == 1)) & (zs >= 0) & (zs < Z))
            def _():
                attend(zs, y)
            return carry

        lax.fori_loop(0, 2, along_z, 0)
        return carry

    lax.fori_loop(0, Z + 1, step, 0)

    def att_copy(h):
        at = pl.ds(h * HEAD_DIM, HEAD_DIM)
        return pltpu.make_async_remote_copy(
            src_ref=att_own.at[:, at], dst_ref=att_other.at[:, at], send_sem=att_send.at[h],
            recv_sem=att_recv.at[h], device_id=other, device_id_type=MESH,
        )

    for h in range(heads):
        done = acc[h] / total[h]
        att_own[:, h * HEAD_DIM:(h + 1) * HEAD_DIM] = done.T.astype(jnp.bfloat16)
        att_copy(h).start()

    w_copy.wait()
    chunk = half // 3
    for c in range(3):
        at = slice(c * chunk, (c + 1) * chunk)
        proj[:, at] = jnp.dot(att_own[...], w_own[:, at], preferred_element_type=jnp.float32)
    lat_copy.wait()
    w_send.wait()
    for h in range(heads):
        att_copy(h).wait()
    outs = []
    for c in range(3):
        at = slice(c * chunk, (c + 1) * chunk)
        full = proj[:, at] + jnp.dot(
            att_other[...], w_other[:, at], preferred_element_type=jnp.float32
        )
        result = lat[:, at].astype(jnp.float32) + gate_ref[at].astype(jnp.float32)[None, :] * full
        mixed[:, at] = result.astype(jnp.bfloat16)
        there_at = pl.ds(c * chunk, chunk)
        copy = pltpu.make_async_copy(mixed.at[:, there_at], out_hbm.at[:, there_at], out_sem.at[c])
        copy.start()
        outs.append(copy)

    def sent(slot, carry):
        zs, ys = slot // Y, slot % Y
        for k in range(len(pieces)):
            for side, goes in enumerate(sends(zs, ys, k)):
                @pl.when(goes)
                def _():
                    piece_copy(slot, k, side).wait_send()
        return carry

    lax.fori_loop(0, n, sent, 0)
    for copy in outs:
        copy.wait()


def local(n, inner, queries, fresh_pairs, stale_pairs, counts, latents, out_weight, gate):
    slots, width = queries.shape
    rows = stale_pairs.shape[1]
    half = latents.shape[1]
    heads = width // HEAD_DIM
    bf16, f32 = jnp.bfloat16, jnp.float32
    anywhere = pl.BlockSpec(memory_space=pl.ANY)
    dma = pltpu.SemaphoreType.DMA
    return pl.pallas_call(
        functools.partial(kernel, n, inner),
        out_shape=jax.ShapeDtypeStruct((slots, half), bf16),
        in_specs=[pl.BlockSpec(memory_space=pltpu.SMEM)] + [anywhere] * 5
        + [pl.BlockSpec(memory_space=pltpu.VMEM)],
        out_specs=anywhere,
        scratch_shapes=[
            pltpu.VMEM((slots, width), bf16),
            pltpu.VMEM((2, slots, width), bf16),
            pltpu.VMEM((n, 2, rows, width), bf16),
            pltpu.VMEM((slots, half), bf16),
            pltpu.VMEM((width, half), bf16),
            pltpu.VMEM((width, half), bf16),
            pltpu.VMEM((heads, 1, slots), f32),
            pltpu.VMEM((heads, 1, slots), f32),
            pltpu.VMEM((heads, HEAD_DIM, slots), f32),
            pltpu.VMEM((slots, width), bf16),
            pltpu.VMEM((slots, width), bf16),
            pltpu.VMEM((slots, half), f32),
            pltpu.VMEM((slots, half), bf16),
            dma((5,)),
            dma((6, 4, n)),
            dma((6, n)),
            dma((2,)),
            dma((heads,)),
            dma((heads,)),
            dma((3,)),
        ],
        compiler_params=pltpu.CompilerParams(
            collective_id=0, has_side_effects=True, vmem_limit_bytes=56 * 2 ** 20
        ),
    )(counts, queries, fresh_pairs, stale_pairs, latents, out_weight, gate)


def solution(mesh):
    n = mesh.shape["patch"]
    root = math.isqrt(n)
    inner = next(size for size in range(root, 0, -1) if n % size == 0)
    placed = (
        P(("grp", "patch"), "head"),
        P(None, ("grp", "patch"), "head"),
        P(None, ("grp", "patch"), "head"),
        P("grp"),
        P(("grp", "patch"), "head"),
        P("head", None),
        P(("grp", "head")),
    )
    return jax.shard_map(
        functools.partial(local, n, inner), mesh=mesh, in_specs=placed,
        out_specs=P(("grp", "patch"), "head"), check_vma=False,
    )
```

```python
import functools
import math

import jax
import jax.numpy as jnp
from jax import lax
from jax.experimental import pallas as pl
from jax.experimental.pallas import tpu as pltpu
from jax.sharding import PartitionSpec as P

HEAD_DIM = 128
MASKED = -1e30
MESH = pl.DeviceIdType.MESH


def kernel(
    n, inner, counts_ref, q_hbm, fresh_hbm, stale_hbm, lat_hbm, w_hbm, gate_ref, out_hbm,
    q, fresh, slots, lat, w_own, w_other, top, total, acc, att_own, att_other, proj, mixed,
    held, shrunk,
    local_sem, send_sem, recv_sem, w_sem, att_send, att_recv, out_sem,
):
    Z, Y = n // inner, inner
    grp, me, core = lax.axis_index("grp"), lax.axis_index("patch"), lax.axis_index("head")
    z, y = me // Y, me % Y
    rows = slots.shape[2]
    width = q.shape[1]
    heads = width // HEAD_DIM
    half = lat.shape[1]
    scale = math.log2(math.e) / HEAD_DIM ** 0.5
    cut = (rows // 3) // 16 * 16
    pieces = ((1, 0, cut, True), (0, 0, cut, False), (0, cut, cut, False), (0, 2 * cut, rows - 2 * cut, False), (1, cut, cut, False), (1, 2 * cut, rows - 2 * cut, False))
    other = (grp, me, 1 - core)

    def there(step):
        return (grp, me + step, core)

    sides = ((z > 0, -Y), (z < Z - 1, Y), (y > 0, -1), (y < Y - 1, 1))

    own_copy = pltpu.make_async_copy(stale_hbm, slots.at[me], local_sem.at[0])
    own_copy.start()
    q_copy = pltpu.make_async_copy(q_hbm, q, local_sem.at[1])
    q_copy.start()
    fresh_copy = pltpu.make_async_copy(fresh_hbm, fresh, local_sem.at[2])
    fresh_copy.start()

    barrier = pltpu.get_barrier_semaphore()
    for there_is, step in sides:
        @pl.when(there_is)
        def _():
            pl.semaphore_signal(barrier, inc=1, device_id=there(step), device_id_type=MESH)
    pl.semaphore_signal(barrier, inc=1, device_id=other, device_id_type=MESH)
    peers = jnp.int32(1)
    for there_is, _step in sides:
        peers = peers + there_is.astype(jnp.int32)
    pl.semaphore_wait(barrier, peers)

    def piece_copy(slot, k, side):
        kind, first, count, _ = pieces[k]
        ref = slots.at[slot, kind, pl.ds(first, count), :]
        return pltpu.make_async_remote_copy(
            src_ref=ref, dst_ref=ref, send_sem=send_sem.at[k, side, slot],
            recv_sem=recv_sem.at[k, slot], device_id=there(sides[side][1]), device_id_type=MESH,
        )

    def sends(zs, ys, k):
        y_first = pieces[k][3]
        down, up = (zs >= z) & (z > 0), (zs <= z) & (z < Z - 1)
        left, right = (ys >= y) & (y > 0), (ys <= y) & (y < Y - 1)
        if y_first:
            return down, up, left & (zs == z), right & (zs == z)
        return down & (ys == y), up & (ys == y), left, right

    def forward(zs, ys, k):
        slot = zs * Y + ys
        for side, goes in enumerate(sends(zs, ys, k)):
            @pl.when(goes)
            def _():
                piece_copy(slot, k, side).start()

    def arrive(zs, ys, k):
        piece_copy(zs * Y + ys, k, 0).wait_recv()
        forward(zs, ys, k)

    own_copy.wait()
    for k in range(len(pieces)):
        forward(z, y, k)

    lat_copy = pltpu.make_async_copy(lat_hbm, lat, local_sem.at[3])
    lat_copy.start()
    mine = pl.ds(pl.multiple_of(core * half, half), half)
    theirs = pl.ds(pl.multiple_of((1 - core) * half, half), half)
    w_copy = pltpu.make_async_copy(w_hbm.at[:, mine], w_own, local_sem.at[4])
    w_copy.start()
    w_send = pltpu.make_async_remote_copy(
        src_ref=w_hbm.at[:, theirs], dst_ref=w_other, send_sem=w_sem.at[0], recv_sem=w_sem.at[1],
        device_id=other, device_id_type=MESH,
    )
    w_send.start()

    low = jnp.int32(0)
    own = jnp.int32(0)
    for p in range(n):
        count = counts_ref[p]
        low = low + jnp.where(p < me, count, 0)
        own = own + jnp.where(p == me, count, 0)
    high = low + own

    def part(key_of, value_of, dead, first):
        for h in range(heads):
            at = slice(h * HEAD_DIM, (h + 1) * HEAD_DIM)
            s = lax.dot_general(
                key_of(at), q[:, at], (((1,), (1,)), ((), ())), preferred_element_type=jnp.float32
            )
            s = jnp.where(dead, MASKED, s)
            peak = jnp.max(s, axis=0, keepdims=True)
            if not first:
                before = top[h]
                peak = jnp.maximum(before, peak)
            weights = jnp.exp2((s - peak) * scale)
            summed = jnp.sum(weights, axis=0, keepdims=True)
            added = lax.dot_general(
                value_of(at), weights.astype(jnp.bfloat16), (((0,), (0,)), ((), ())),
                preferred_element_type=jnp.float32,
            )
            top[h] = peak
            if first:
                total[h] = summed
                acc[h] = added
            else:
                shrink = jnp.exp2((before - peak) * scale)
                total[h] = total[h] * shrink + summed
                acc[h] = acc[h] * shrink + added

    def attend(zs, ys):
        slot = zs * Y + ys
        row = slot * rows + lax.broadcasted_iota(jnp.int32, (rows, q.shape[0]), 0)
        dead = (row >= low) & (row < high)
        part(lambda at: slots[slot, 0, :, at], lambda at: slots[slot, 1, :, at], dead, False)

    def weigh(zs, ys):
        slot = zs * Y + ys
        row = slot * rows + lax.broadcasted_iota(jnp.int32, (rows, q.shape[0]), 0)
        dead = (row >= low) & (row < high)
        for h in range(heads):
            at = slice(h * HEAD_DIM, (h + 1) * HEAD_DIM)
            s = lax.dot_general(
                slots[slot, 0, :, at], q[:, at], (((1,), (1,)), ((), ())),
                preferred_element_type=jnp.float32,
            )
            s = jnp.where(dead, MASKED, s)
            before = top[h]
            peak = jnp.maximum(before, jnp.max(s, axis=0, keepdims=True))
            weights = jnp.exp2((s - peak) * scale)
            shrink = jnp.exp2((before - peak) * scale)
            top[h] = peak
            total[h] = total[h] * shrink + jnp.sum(weights, axis=0, keepdims=True)
            shrunk[h] = shrink
            held[h] = weights.astype(jnp.bfloat16)

    def gather_values(zs, ys):
        slot = zs * Y + ys
        for h in range(heads):
            at = slice(h * HEAD_DIM, (h + 1) * HEAD_DIM)
            added = lax.dot_general(
                slots[slot, 1, :, at], held[h], (((0,), (0,)), ((), ())),
                preferred_element_type=jnp.float32,
            )
            acc[h] = acc[h] * shrunk[h] + added

    q_copy.wait()
    fresh_copy.wait()
    place = lax.broadcasted_iota(jnp.int32, (fresh.shape[1], q.shape[0]), 0)
    part(lambda at: fresh[0, :, at], lambda at: fresh[1, :, at], place >= own, True)

    def step(d, carry):
        for k in range(len(pieces)):
            for sign in (-1, 1):
                zs = z + sign * d

                @pl.when((d >= 1) & (zs >= 0) & (zs < Z))
                def _():
                    arrive(zs, y, k)

        e = d - 1

        def along_y(t, carry):
            dy, sz, sy = t // 4 + 1, 2 * ((t // 2) % 2) - 1, 2 * (t % 2) - 1
            zs, ys = z + sz * e, y + sy * dy
            once = (e >= 1) | ((e == 0) & (sz == 1))

            @pl.when(once & (zs >= 0) & (zs < Z) & (ys >= 0) & (ys < Y))
            def _():
                for k in range(4):
                    arrive(zs, ys, k)
                weigh(zs, ys)
                for k in range(4, len(pieces)):
                    arrive(zs, ys, k)
                gather_values(zs, ys)
            return carry

        lax.fori_loop(0, 4 * (Y - 1), along_y, 0)

        def along_z(t, carry):
            zs = z + (2 * t - 1) * d

            @pl.when(((d >= 1) | (t == 1)) & (zs >= 0) & (zs < Z))
            def _():
                attend(zs, y)
            return carry

        lax.fori_loop(0, 2, along_z, 0)
        return carry

    lax.fori_loop(0, Z + 1, step, 0)

    def att_copy(h):
        at = pl.ds(h * HEAD_DIM, HEAD_DIM)
        return pltpu.make_async_remote_copy(
            src_ref=att_own.at[:, at], dst_ref=att_other.at[:, at], send_sem=att_send.at[h],
            recv_sem=att_recv.at[h], device_id=other, device_id_type=MESH,
        )

    for h in range(heads):
        done = acc[h] / total[h]
        att_own[:, h * HEAD_DIM:(h + 1) * HEAD_DIM] = done.T.astype(jnp.bfloat16)
        att_copy(h).start()

    w_copy.wait()
    chunk = half // 3
    for c in range(3):
        at = slice(c * chunk, (c + 1) * chunk)
        proj[:, at] = jnp.dot(att_own[...], w_own[:, at], preferred_element_type=jnp.float32)
    lat_copy.wait()
    w_send.wait()
    for h in range(heads):
        att_copy(h).wait()
    outs = []
    for c in range(3):
        at = slice(c * chunk, (c + 1) * chunk)
        full = proj[:, at] + jnp.dot(
            att_other[...], w_other[:, at], preferred_element_type=jnp.float32
        )
        result = lat[:, at].astype(jnp.float32) + gate_ref[at].astype(jnp.float32)[None, :] * full
        mixed[:, at] = result.astype(jnp.bfloat16)
        there_at = pl.ds(c * chunk, chunk)
        copy = pltpu.make_async_copy(mixed.at[:, there_at], out_hbm.at[:, there_at], out_sem.at[c])
        copy.start()
        outs.append(copy)

    def sent(slot, carry):
        zs, ys = slot // Y, slot % Y
        for k in range(len(pieces)):
            for side, goes in enumerate(sends(zs, ys, k)):
                @pl.when(goes)
                def _():
                    piece_copy(slot, k, side).wait_send()
        return carry

    lax.fori_loop(0, n, sent, 0)
    for copy in outs:
        copy.wait()


def local(n, inner, queries, fresh_pairs, stale_pairs, counts, latents, out_weight, gate):
    slots, width = queries.shape
    rows = stale_pairs.shape[1]
    half = latents.shape[1]
    heads = width // HEAD_DIM
    bf16, f32 = jnp.bfloat16, jnp.float32
    anywhere = pl.BlockSpec(memory_space=pl.ANY)
    dma = pltpu.SemaphoreType.DMA
    return pl.pallas_call(
        functools.partial(kernel, n, inner),
        out_shape=jax.ShapeDtypeStruct((slots, half), bf16),
        in_specs=[pl.BlockSpec(memory_space=pltpu.SMEM)] + [anywhere] * 5
        + [pl.BlockSpec(memory_space=pltpu.VMEM)],
        out_specs=anywhere,
        scratch_shapes=[
            pltpu.VMEM((slots, width), bf16),
            pltpu.VMEM((2, slots, width), bf16),
            pltpu.VMEM((n, 2, rows, width), bf16),
            pltpu.VMEM((slots, half), bf16),
            pltpu.VMEM((width, half), bf16),
            pltpu.VMEM((width, half), bf16),
            pltpu.VMEM((heads, 1, slots), f32),
            pltpu.VMEM((heads, 1, slots), f32),
            pltpu.VMEM((heads, HEAD_DIM, slots), f32),
            pltpu.VMEM((slots, width), bf16),
            pltpu.VMEM((slots, width), bf16),
            pltpu.VMEM((slots, half), f32),
            pltpu.VMEM((slots, half), bf16),
            pltpu.VMEM((heads, rows, slots), bf16),
            pltpu.VMEM((heads, 1, slots), f32),
            dma((5,)),
            dma((6, 4, n)),
            dma((6, n)),
            dma((2,)),
            dma((heads,)),
            dma((heads,)),
            dma((3,)),
        ],
        compiler_params=pltpu.CompilerParams(
            collective_id=0, has_side_effects=True, vmem_limit_bytes=56 * 2 ** 20
        ),
    )(counts, queries, fresh_pairs, stale_pairs, latents, out_weight, gate)


def solution(mesh):
    n = mesh.shape["patch"]
    root = math.isqrt(n)
    inner = next(size for size in range(root, 0, -1) if n % size == 0)
    placed = (
        P(("grp", "patch"), "head"),
        P(None, ("grp", "patch"), "head"),
        P(None, ("grp", "patch"), "head"),
        P("grp"),
        P(("grp", "patch"), "head"),
        P("head", None),
        P(("grp", "head")),
    )
    return jax.shard_map(
        functools.partial(local, n, inner), mesh=mesh, in_specs=placed,
        out_specs=P(("grp", "patch"), "head"), check_vma=False,
    )
```
